32 devices in a mesh: dp: 4 (over y, x), feat: 8 (over z, core).
Axes of the slice: x: 2, y: 2, z: 4, core: 2. Of those that a mesh axis runs over, the one named last changes fastest.
Arguments:
- tokens: bfloat16 [512, 16384], P('dp', 'feat'), may hold values from -6 to 6
- columns: int32 [256, 16], P('feat'), may hold values from 0 to 127, all different within a row
- weight: bfloat16 [256, 16, 128, 128], P('feat', None, 'dp'), may hold values from -0.125 to 0.125
- cotangent: bfloat16 [512, 32768], P('dp', 'feat'), may hold values from -6 to 6
Outputs:
- hidden: bfloat16 [512, 32768], P('dp', 'feat')
- input_grad: bfloat16 [512, 16384], P('dp', 'feat')
- weight_grad: bfloat16 [256, 16, 128, 128], P('feat', None, 'dp')
The draws below stay inside these ranges and needn't reach their ends.
Inputs may be any that keep to these rules, and one draw needn't show every extreme that they name: `columns`: the 16 entries of a row are distinct input blocks; every input block is named by some row.
All inputs are finite; a program needn't handle non-finite values.
Results may differ from the reference program's by a relative error of at most 0.019.
Values may be sent and summed in bfloat16 or wider, within the bound.
A program may use at most 128 MiB of HBM per device.

```python
import jax
import jax.numpy as jnp
from jax import lax

BLK = 128
D = 16384
H = 32768
NNZ = 16
TOK_DEV = 128
TOKENS = 512
DB = 128
HB = 256
N_DP = 4
N_FEAT = 8


def level_of(stream_key, shape, shards, low, high):
    def one(dim, blocks):
        heights = jax.random.uniform(jax.random.fold_in(jax.random.fold_in(stream_key, 6), dim), (blocks,), jnp.float32, low / len(shards), high / len(shards))
        return jnp.repeat(jnp.exp(heights), shape[dim] // blocks).reshape((-1,) + (1,) * (len(shape) - dim - 1))

    factor_of = one(*shards[0])
    for cut in shards[1:]:
        factor_of = factor_of * one(*cut)
    return factor_of


def distinct(own_key, rows, amount, top, lift):
    ranking = jax.random.permutation(jax.random.fold_in(own_key, 1), amount)
    favour = ranking
    for power in range(3):
        favour = favour * favour // amount
    favour = favour * lift // amount
    chance = jax.random.randint(jax.random.fold_in(own_key, 2), (rows, amount), 0, 4096) + favour
    sure = jax.random.permutation(jax.random.fold_in(own_key, 3), rows)[jnp.arange(amount) % rows]
    chance = jnp.where(jnp.arange(rows)[:, None] == sure[None, :], 1 << 14, chance)
    merit = chance * amount + jnp.arange(amount)
    return lax.top_k(merit.astype(jnp.int32), top)[1].astype(jnp.int32)


def noise(own_key, extent, scale, reach, shards=(), kind=jnp.bfloat16):
    gain = level_of(own_key, extent, shards, -0.22, 0.18) if shards else 1.0
    entries = jax.random.normal(own_key, extent, jnp.float32) * scale * gain
    return jnp.minimum(jnp.maximum(entries, -reach), reach).astype(kind)


def setup_inputs(seed: int = 0) -> dict:
    splits = jax.random.split(jax.random.key(seed), 5)
    tokens = noise(splits[0], (TOKENS, D), 1.0, 6.0, ((0, 4), (1, 8)))
    columns = distinct(splits[1], HB, D // BLK, NNZ, 2048)
    weight = noise(splits[2], (HB, NNZ, BLK, BLK), (NNZ * BLK) ** -0.5, 0.125, ((0, 8), (2, 4)))
    cotangent = noise(splits[3], (TOKENS, H), 1.0, 6.0, ((0, 4), (1, 8)))
    return {"tokens": tokens, "columns": columns, "weight": weight, "cotangent": cotangent}


def gelu_tanh(value):
    return jax.nn.gelu(value, approximate=True)

def reference(tokens, columns, weight, cotangent):
    total_tok = tokens.shape[0]
    blocks = tokens.reshape(total_tok, DB, BLK)
    rows_dev = HB // N_FEAT
    block_ids = jnp.arange(DB, dtype=jnp.int32)

    def group(carry, index):
        start = (index * rows_dev).astype(jnp.int32)
        cols = lax.dynamic_slice_in_dim(columns, start, rows_dev, 0)
        wblk = lax.dynamic_slice_in_dim(weight, start, rows_dev, 0).astype(jnp.float32)
        cot = lax.dynamic_slice_in_dim(cotangent, (start * BLK).astype(jnp.int32), rows_dev * BLK, 1)
        picked = blocks[:, cols.reshape(-1), :].reshape(total_tok, rows_dev, NNZ, BLK).astype(jnp.float32)
        pre = jnp.einsum('trsk,rsuk->tru', picked, wblk)
        act, pull = jax.vjp(gelu_tanh, pre)
        hidden = act.astype(jnp.bfloat16).reshape(total_tok, rows_dev * BLK)
        grad_pre = pull(cot.reshape(total_tok, rows_dev, BLK).astype(jnp.float32))[0].astype(jnp.bfloat16)
        gp = grad_pre.astype(jnp.float32)
        terms = jnp.einsum('gtru,gtrsk->grsuk', gp.reshape(N_DP, TOK_DEV, rows_dev, BLK), picked.reshape(N_DP, TOK_DEV, rows_dev, NNZ, BLK))
        wgrad = lax.optimization_barrier(jnp.sum(terms.astype(jnp.bfloat16).astype(jnp.float32), axis=0)).astype(jnp.bfloat16)
        parts = jnp.einsum('tru,rsuk->trsk', gp, wblk).reshape(total_tok, rows_dev * NNZ, BLK)
        onehot = (cols.reshape(-1)[:, None] == block_ids[None, :]).astype(jnp.float32)
        spread = jnp.einsum('tqk,qb->tbk', parts, onehot, precision=lax.Precision.HIGHEST)
        spread = spread.astype(jnp.bfloat16).astype(jnp.float32).reshape(total_tok, D)
        return (carry + spread, (hidden, wgrad))
    acc, (hid, wgr) = lax.scan(group, jnp.zeros((total_tok, D), jnp.float32), jnp.arange(N_FEAT, dtype=jnp.int32))
    hidden = jnp.transpose(hid, (1, 0, 2)).reshape(total_tok, H)
    weight_grad = wgr.reshape(HB, NNZ, BLK, BLK)
    return (hidden, acc.astype(jnp.bfloat16), weight_grad)
```

```python
import functools

import jax
import jax.numpy as jnp
from jax import lax
from jax.experimental import pallas as pl
from jax.experimental.pallas import tpu as pltpu
from jax.sharding import PartitionSpec as P

MESH = pl.DeviceIdType.MESH
LINE = 4


def gelu_tanh(value):
    return jax.nn.gelu(value, approximate=True)


def on_device(tokens, columns, weight, cotangent):
    tok_rows = tokens.shape[0]
    local_rows = weight.shape[0]
    slots = weight.shape[1]
    side = weight.shape[3]
    feat_count = lax.axis_size("feat")
    gathered = lax.all_gather(tokens, "feat", axis=1, tiled=True)
    block_count = gathered.shape[1] // side
    flat_cols = columns.reshape(-1)
    picked = gathered.reshape(tok_rows, block_count, side)[:, flat_cols, :].reshape(
        tok_rows, local_rows, slots, side
    )
    full_weight = lax.all_gather(weight, "dp", axis=2, tiled=True)
    pre = jnp.einsum("trsk,rsuk->tru", picked, full_weight, preferred_element_type=jnp.float32)
    act, pull = jax.vjp(gelu_tanh, pre)
    hidden = act.astype(jnp.bfloat16).reshape(tok_rows, local_rows * side)
    grad_pre = pull(cotangent.reshape(tok_rows, local_rows, side).astype(jnp.float32))[0].astype(
        jnp.bfloat16
    )
    weight_terms = jnp.einsum(
        "tru,trsk->rsuk", grad_pre, picked, preferred_element_type=jnp.float32
    )
    weight_grad = lax.psum_scatter(
        weight_terms.astype(jnp.bfloat16), "dp", scatter_dimension=2, tiled=True
    )
    partial_grad = jnp.einsum(
        "tru,rsuk->trsk", grad_pre, full_weight, preferred_element_type=jnp.float32
    )
    onehot = (flat_cols[:, None] == jnp.arange(block_count, dtype=jnp.int32)[None, :]).astype(
        jnp.float32
    )
    spread = jnp.einsum(
        "tqk,qb->tbk",
        partial_grad.reshape(tok_rows, local_rows * slots, side),
        onehot,
        precision=lax.Precision.HIGHEST,
    )
    outgoing = spread.reshape(tok_rows, block_count * side).astype(jnp.bfloat16)
    returned = lax.all_to_all(outgoing, "feat", split_axis=1, concat_axis=0, tiled=True)
    input_grad = jnp.sum(
        returned.reshape(feat_count, tok_rows, -1).astype(jnp.float32), axis=0
    ).astype(jnp.bfloat16)
    return (hidden, input_grad, weight_grad)


def place():
    i, f = lax.axis_index("dp"), lax.axis_index("feat")
    z, c = f // 2, f % 2
    px = i + 1 - 2 * (i % 2)
    py = i + 2 - 4 * (i // 2)
    return i, f, z, c, px, py, 3 - i


def line_order(z):
    m = z // 2
    zz = z + m * (3 - 2 * z)
    near = [zz, 1 - zz, 2 + 0 * zz, 3 + 0 * zz]
    return [q + m * (3 - 2 * q) for q in near]


def enter(i, f, z, px, py, pd):
    barrier = pltpu.get_barrier_semaphore()

    def greet(**where):
        pl.semaphore_signal(barrier, inc=1, device_id=where, device_id_type=MESH)

    for p in (px, py, pd):
        greet(dp=p, feat=f)
    greet(dp=i, feat=f + 1 - 2 * (f % 2))

    @pl.when(z > 0)
    def _():
        greet(dp=i, feat=f - 2)

    @pl.when(z < LINE - 1)
    def _():
        greet(dp=i, feat=f + 2)

    pl.semaphore_wait(barrier, 5 + z * (LINE - 1 - z) // (LINE - 2))


def rcopy(src, dst, send, recv, **where):
    return pltpu.make_async_remote_copy(
        src_ref=src, dst_ref=dst, send_sem=send, recv_sem=recv, device_id=where, device_id_type=MESH
    )


def gather_kernel(
    tokens, cot, tok_all, cot_all, own, a2a_s, a2a_r, up_s, dn_s, line_r, xy_s, xy_r, dg_s, dg_r,
    sib_s, sib_r,
):
    i, f, z, c, px, py, pd = place()
    half = tokens.shape[0] // 2
    order = line_order(z)
    sib = f + 1 - 2 * c
    enter(i, f, z, px, py, pd)

    mine = pltpu.make_async_copy(tokens, tok_all.at[i, f], own.at[0])
    mine.start()
    keep = pltpu.make_async_copy(cot.at[i], cot_all.at[i], own.at[1])
    keep.start()

    def blk(who, zp):
        return tok_all.at[who, 2 * zp + c]

    def src(k):
        return tokens if k == 0 else blk(i, order[k])

    def up(k):
        return rcopy(src(k), blk(i, order[k]), up_s.at[k], line_r.at[order[k]], dp=i, feat=f + 2)

    def down(k):
        return rcopy(src(k), blk(i, order[k]), dn_s.at[k], line_r.at[order[k]], dp=i, feat=f - 2)

    def across(k, n):
        return rcopy(
            src(k), blk(i, order[k]), xy_s.at[n, k], xy_r.at[n, k], dp=(px, py)[n], feat=f
        )

    def corner(k, n):
        rows = pl.ds(n * half, half)
        ref = blk((px, py)[n], order[k]).at[rows]
        return rcopy(ref, ref, dg_s.at[n, k], dg_r.at[n, k], dp=(py, px)[n], feat=f)

    def twin(k, w):
        who = (i, px, py, pd)[w]
        ref = blk(who, order[k])
        s = src(k) if w == 0 else ref
        return rcopy(s, ref, sib_s.at[w, k], sib_r.at[w, k], dp=i, feat=sib)

    def exchange(n):
        p = (px, py, pd)[n]
        return rcopy(cot.at[p], cot_all.at[i], a2a_s.at[n], a2a_r.at[n], dp=p, feat=f)

    def goes_up(k):
        return jnp.logical_and(order[k] <= z, z < LINE - 1)

    def goes_down(k):
        return jnp.logical_and(order[k] >= z, z > 0)

    for k in range(LINE + 2):
        if k < LINE:
            if k > 0:
                pltpu.make_async_copy(
                    blk(i, order[k]), blk(i, order[k]), line_r.at[order[k]]
                ).wait()
            pl.when(goes_up(k))(lambda: up(k).start())
            pl.when(goes_down(k))(lambda: down(k).start())
            for n in range(2):
                across(k, n).start()
            twin(k, 0).start()
        if 1 <= k <= LINE:
            for n in range(2):
                across(k - 1, n).wait_recv()
                corner(k - 1, n).start()
                twin(k - 1, 1 + n).start()
        if k >= 2:
            for n in range(2):
                corner(k - 2, n).wait_recv()
            twin(k - 2, 3).start()
        if k == 1:
            for n in range(3):
                exchange(n).start()

    for n in range(3):
        exchange(n).wait()
    mine.wait()
    keep.wait()
    for k in range(LINE):
        pl.when(goes_up(k))(lambda: up(k).wait_send())
        pl.when(goes_down(k))(lambda: down(k).wait_send())
        for n in range(2):
            across(k, n).wait_send()
            corner(k, n).wait_send()
        for w in range(4):
            twin(k, w).wait()


def spread_kernel(inv, weight, wd):
    f = pl.program_id(0)
    rows, slots, units, side = weight.shape
    per = wd.shape[2] // side

    def row(r, carry):
        for b in range(per):
            s = inv[r, f * per + b]
            val = weight[r, jnp.minimum(s, slots - 1)]
            val = jnp.where(s < slots, val, jnp.zeros_like(val))
            wd[0, pl.ds(pl.multiple_of(r * units, units), units), b * side : (b + 1) * side] = val
        return carry

    lax.fori_loop(0, rows, row, 0)


def local_kernel(cols, tok, weight, cot, hid, wgrad, grad_t, picked):
    step = pl.program_id(0)
    n, slots, units, side = weight.shape
    groups, _, rows, wide = tok.shape
    per = wide // side
    grads = []
    for a in range(n):
        for s in range(slots):
            b = cols[step * n + a, s]
            lanes = pl.ds(pl.multiple_of((b % per) * side, side), side)
            for g in range(groups):
                picked[a % 2, g * rows : (g + 1) * rows, s * side : (s + 1) * side] = tok[
                    g, b // per, :, lanes
                ]
        w = jnp.concatenate([weight[a, s] for s in range(slots)], axis=1)
        x = picked.at[a % 2]
        v = lax.dot_general(w, x[...], (((1,), (1,)), ((), ())), preferred_element_type=jnp.float32)
        k0, k1 = 0.7978845608028654, 0.044715
        th = jnp.tanh(k0 * (v + k1 * v * v * v))
        act = (0.5 * v * (1.0 + th)).astype(jnp.bfloat16)
        slope = 0.5 * (1.0 + th) + 0.5 * v * (1.0 - th * th) * (k0 * (1.0 + 3.0 * k1 * v * v))
        ct = jnp.concatenate([cot[g, a] for g in range(groups)], axis=1).astype(jnp.float32)
        grad = ct * slope
        grads.append(grad)
        grad = grad.astype(jnp.bfloat16)
        for g in range(groups):
            hid[g, a] = act[:, g * rows : (g + 1) * rows]
        wg = jnp.dot(grad, x[...], preferred_element_type=jnp.float32).astype(jnp.bfloat16)
        for s in range(slots):
            wgrad[a, s] = wg[:, s * side : (s + 1) * side]
    grad_t[...] = jnp.concatenate(grads, axis=0).T.astype(jnp.bfloat16)


def scatter_kernel(
    grad_t, wd, hid, out, hid_all, wbuf, part, sibbuf, xhalf, yhalf, xfull, yfull, upbuf, dnbuf,
    own, wsem, a2a_s, a2a_r, sib_s, sib_r, half_s, half_r, full_s, full_r, up_s, up_r, dn_s, dn_r,
):
    i, f, z, c, px, py, pd = place()
    groups, rows, wide = sibbuf.shape[1:]
    half = rows // 2
    order = line_order(z)[::-1]
    sib = f + 1 - 2 * c
    tile = 256

    def fetch(q):
        k, own_side = q // 2, q % 2
        col = 2 * order[k] + (c if own_side else 1 - c)
        return pltpu.make_async_copy(wd.at[col], wbuf.at[q % 2], wsem.at[q % 2])

    fetch(0).start()
    enter(i, f, z, px, py, pd)
    keep = pltpu.make_async_copy(hid.at[i], hid_all.at[i], own)
    keep.start()

    def exchange(n):
        p = (px, py, pd)[n]
        return rcopy(hid.at[p], hid_all.at[i], a2a_s.at[n], a2a_r.at[n], dp=p, feat=f)

    def work(q):
        k = q // 2
        fetch(q).wait()
        if q + 1 < 2 * LINE:
            fetch(q + 1).start()

        def body(n, carry):
            lanes = pl.ds(pl.multiple_of(n * tile, tile), tile)
            res = jnp.dot(
                grad_t[...], wbuf[q % 2, :, lanes], preferred_element_type=jnp.float32
            ).astype(jnp.bfloat16)
            for g in range(groups):
                part[q % 2, k, g, :, lanes] = res[g * rows : (g + 1) * rows]
            return carry

        lax.fori_loop(0, wide // tile, body, 0)

    def add(dst, *others):
        def body(n, carry):
            at = pl.ds(pl.multiple_of(n * 16, 16), 16)
            total = dst[at].astype(jnp.float32)
            for o in others:
                total = total + o[at].astype(jnp.float32)
            dst[at] = total.astype(jnp.bfloat16)
            return carry

        lax.fori_loop(0, dst.shape[0] // 16, body, 0)

    def twin(k):
        return rcopy(part.at[0, k], sibbuf.at[k], sib_s.at[k], sib_r.at[k], dp=i, feat=sib)

    first, second = pl.ds(0, half), pl.ds(half, half)

    def corner(k, n):
        rows_n = (first, second)[n]
        return rcopy(
            part.at[1, k, pd, rows_n], (xhalf, yhalf)[n].at[k], half_s.at[n, k], half_r.at[n, k],
            dp=(px, py)[n], feat=f,
        )

    def across(k, n):
        p = (px, py)[n]
        return rcopy(
            part.at[1, k, p], (xfull, yfull)[n].at[k], full_s.at[n, k], full_r.at[n, k],
            dp=p, feat=f,
        )

    def up(k):
        return rcopy(
            part.at[1, k, i], upbuf.at[order[k]], up_s.at[k], up_r.at[order[k]], dp=i, feat=f + 2
        )

    def down(k):
        return rcopy(
            part.at[1, k, i], dnbuf.at[order[k]], dn_s.at[k], dn_r.at[order[k]], dp=i, feat=f - 2
        )

    def got(buf, sem, k):
        ref = buf.at[order[k]]
        pltpu.make_async_copy(ref, ref, sem.at[order[k]]).wait()

    def from_below(k):
        return jnp.logical_and(order[k] >= z, z > 0)

    def from_above(k):
        return jnp.logical_and(order[k] <= z, z < LINE - 1)

    for step in range(LINE + 3):
        k = step
        if k < LINE:
            work(2 * k)
            twin(k).start()
            work(2 * k + 1)
            if k == 0:
                for n in range(3):
                    exchange(n).start()
            twin(k).wait_recv()
            for g in (pd, px, py, i):
                add(part.at[1, k, g], sibbuf.at[k, g])
                if g is pd:
                    corner(k, 0).start()
                    corner(k, 1).start()
        k = step - 1
        if 0 <= k < LINE:
            corner(k, 0).wait_recv()
            add(part.at[1, k, py, first], xhalf.at[k])
            across(k, 1).start()
            corner(k, 1).wait_recv()
            add(part.at[1, k, px, second], yhalf.at[k])
            across(k, 0).start()
        k = step - 2
        if 0 <= k < LINE:
            across(k, 0).wait_recv()
            across(k, 1).wait_recv()
            add(part.at[1, k, i], xfull.at[k], yfull.at[k])
        k = step - 3
        if 0 <= k < LINE:
            mine = part.at[1, k, i]

            @pl.when(from_below(k))
            def _():
                got(upbuf, up_r, k)
                add(mine, upbuf.at[order[k]])

            @pl.when(from_above(k))
            def _():
                got(dnbuf, dn_r, k)
                add(mine, dnbuf.at[order[k]])

            if k < LINE - 1:
                pl.when(order[k] > z)(lambda: up(k).start())
                pl.when(order[k] < z)(lambda: down(k).start())

    done = pltpu.make_async_copy(part.at[1, LINE - 1, i], out, wsem.at[0])
    done.start()
    for n in range(3):
        exchange(n).wait()
    keep.wait()
    for k in range(LINE):
        twin(k).wait_send()
        for n in range(2):
            corner(k, n).wait_send()
            across(k, n).wait_send()
        if k < LINE - 1:
            pl.when(order[k] > z)(lambda: up(k).wait_send())
            pl.when(order[k] < z)(lambda: down(k).wait_send())
    done.wait()


def token_plan(tokens, columns, weight, cotangent):
    rows, wide = tokens.shape
    local, slots, units, side = weight.shape
    n_dp, n_feat = lax.axis_size("dp"), lax.axis_size("feat")
    bf = jnp.bfloat16
    dma = pltpu.SemaphoreType.DMA
    anywhere = pl.BlockSpec(memory_space=pl.ANY)
    inside = pl.BlockSpec(memory_space=pltpu.VMEM)
    blocks = n_feat * wide // side
    total = n_dp * rows

    cot_t = cotangent.reshape(rows, local, n_dp, units).transpose(2, 1, 3, 0)
    tok_all, cot_all = pl.pallas_call(
        gather_kernel,
        out_shape=(
            jax.ShapeDtypeStruct((n_dp, n_feat, rows, wide), bf),
            jax.ShapeDtypeStruct(cot_t.shape, bf),
        ),
        in_specs=[anywhere] * 2,
        out_specs=(anywhere,) * 2,
        scratch_shapes=[
            dma((2,)), dma((3,)), dma((3,)), dma((LINE,)), dma((LINE,)), dma((LINE,)),
            dma((2, LINE)), dma((2, LINE)), dma((2, LINE)), dma((2, LINE)),
            dma((4, LINE)), dma((4, LINE)),
        ],
        compiler_params=pltpu.CompilerParams(collective_id=0, has_side_effects=True),
        name="gather",
    )(tokens, cot_t)

    hit = columns[:, :, None] == jnp.arange(blocks, dtype=jnp.int32)
    inv = jnp.min(jnp.where(hit, jnp.arange(slots, dtype=jnp.int32)[:, None], slots), axis=1)
    dense = pl.pallas_call(
        spread_kernel,
        out_shape=jax.ShapeDtypeStruct((n_feat, local * units, wide), bf),
        grid_spec=pltpu.PrefetchScalarGridSpec(
            num_scalar_prefetch=1,
            grid=(n_feat,),
            in_specs=[inside],
            out_specs=pl.BlockSpec((1, local * units, wide), lambda f, inv: (f, 0, 0)),
        ),
        compiler_params=pltpu.CompilerParams(vmem_limit_bytes=32 * 2**20),
        name="spread",
    )(inv, weight)

    n = side // units
    hid_t, weight_grad, grad_t = pl.pallas_call(
        local_kernel,
        out_shape=(
            jax.ShapeDtypeStruct(cot_t.shape, bf),
            jax.ShapeDtypeStruct(weight.shape, bf),
            jax.ShapeDtypeStruct((total, local * units), bf),
        ),
        grid_spec=pltpu.PrefetchScalarGridSpec(
            num_scalar_prefetch=1,
            grid=(local // n,),
            in_specs=[
                inside,
                pl.BlockSpec((n, slots, units, side), lambda r, c: (r, 0, 0, 0)),
                pl.BlockSpec((n_dp, n, units, rows), lambda r, c: (0, r, 0, 0)),
            ],
            out_specs=(
                pl.BlockSpec((n_dp, n, units, rows), lambda r, c: (0, r, 0, 0)),
                pl.BlockSpec((n, slots, units, side), lambda r, c: (r, 0, 0, 0)),
                pl.BlockSpec((total, n * units), lambda r, c: (0, r)),
            ),
            scratch_shapes=[pltpu.VMEM((2, total, slots * side), bf)],
        ),
        compiler_params=pltpu.CompilerParams(vmem_limit_bytes=48 * 2**20),
        name="local",
    )(columns, tok_all, weight, cot_all)

    input_grad, hid_all = pl.pallas_call(
        scatter_kernel,
        out_shape=(
            jax.ShapeDtypeStruct((rows, wide), bf),
            jax.ShapeDtypeStruct(cot_t.shape, bf),
        ),
        in_specs=[inside, anywhere, anywhere],
        out_specs=(anywhere,) * 2,
        scratch_shapes=[
            pltpu.VMEM((2, local * units, wide), bf),
            pltpu.VMEM((2, LINE, n_dp, rows, wide), bf),
            pltpu.VMEM((LINE, n_dp, rows, wide), bf),
            pltpu.VMEM((LINE, rows // 2, wide), bf),
            pltpu.VMEM((LINE, rows // 2, wide), bf),
            pltpu.VMEM((LINE, rows, wide), bf),
            pltpu.VMEM((LINE, rows, wide), bf),
            pltpu.VMEM((LINE, rows, wide), bf),
            pltpu.VMEM((LINE, rows, wide), bf),
            dma(()), dma((2,)), dma((3,)), dma((3,)), dma((LINE,)), dma((LINE,)),
            dma((2, LINE)), dma((2, LINE)), dma((2, LINE)), dma((2, LINE)),
            dma((LINE,)), dma((LINE,)), dma((LINE,)), dma((LINE,)),
        ],
        compiler_params=pltpu.CompilerParams(
            collective_id=1, has_side_effects=True, vmem_limit_bytes=56 * 2**20
        ),
        name="scatter",
    )(grad_t, dense, hid_t)
    hidden = hid_all.transpose(3, 1, 0, 2).reshape(rows, local * side)
    return (hidden, input_grad, weight_grad)


def solution(mesh):
    in_specs = (P("dp", "feat"), P("feat", None), P("feat", None, "dp", None), P("dp", "feat"))
    out_specs = (P("dp", "feat"), P("dp", "feat"), P("feat", None, "dp", None))
    square = mesh.shape["dp"] == 4 and mesh.shape["feat"] == 2 * LINE
    return jax.shard_map(
        token_plan if square else on_device,
        mesh=mesh, in_specs=in_specs, out_specs=out_specs, check_vma=False,
    )
```

```python
import functools

import jax
import jax.numpy as jnp
from jax import lax
from jax.experimental import pallas as pl
from jax.experimental.pallas import tpu as pltpu
from jax.sharding import PartitionSpec as P

MESH = pl.DeviceIdType.MESH
LINE = 4


def gelu_tanh(value):
    return jax.nn.gelu(value, approximate=True)


def on_device(tokens, columns, weight, cotangent):
    tok_rows = tokens.shape[0]
    local_rows = weight.shape[0]
    slots = weight.shape[1]
    side = weight.shape[3]
    feat_count = lax.axis_size("feat")
    gathered = lax.all_gather(tokens, "feat", axis=1, tiled=True)
    block_count = gathered.shape[1] // side
    flat_cols = columns.reshape(-1)
    picked = gathered.reshape(tok_rows, block_count, side)[:, flat_cols, :].reshape(
        tok_rows, local_rows, slots, side
    )
    full_weight = lax.all_gather(weight, "dp", axis=2, tiled=True)
    pre = jnp.einsum("trsk,rsuk->tru", picked, full_weight, preferred_element_type=jnp.float32)
    act, pull = jax.vjp(gelu_tanh, pre)
    hidden = act.astype(jnp.bfloat16).reshape(tok_rows, local_rows * side)
    grad_pre = pull(cotangent.reshape(tok_rows, local_rows, side).astype(jnp.float32))[0].astype(
        jnp.bfloat16
    )
    weight_terms = jnp.einsum(
        "tru,trsk->rsuk", grad_pre, picked, preferred_element_type=jnp.float32
    )
    weight_grad = lax.psum_scatter(
        weight_terms.astype(jnp.bfloat16), "dp", scatter_dimension=2, tiled=True
    )
    partial_grad = jnp.einsum(
        "tru,rsuk->trsk", grad_pre, full_weight, preferred_element_type=jnp.float32
    )
    onehot = (flat_cols[:, None] == jnp.arange(block_count, dtype=jnp.int32)[None, :]).astype(
        jnp.float32
    )
    spread = jnp.einsum(
        "tqk,qb->tbk",
        partial_grad.reshape(tok_rows, local_rows * slots, side),
        onehot,
        precision=lax.Precision.HIGHEST,
    )
    outgoing = spread.reshape(tok_rows, block_count * side).astype(jnp.bfloat16)
    returned = lax.all_to_all(outgoing, "feat", split_axis=1, concat_axis=0, tiled=True)
    input_grad = jnp.sum(
        returned.reshape(feat_count, tok_rows, -1).astype(jnp.float32), axis=0
    ).astype(jnp.bfloat16)
    return (hidden, input_grad, weight_grad)


def place():
    i, f = lax.axis_index("dp"), lax.axis_index("feat")
    z, c = f // 2, f % 2
    px = i + 1 - 2 * (i % 2)
    py = i + 2 - 4 * (i // 2)
    return i, f, z, c, px, py, 3 - i


def line_order(z):
    m = z // 2
    zz = z + m * (3 - 2 * z)
    near = [zz, 1 - zz, 2 + 0 * zz, 3 + 0 * zz]
    return [q + m * (3 - 2 * q) for q in near]


def enter(i, f, z, px, py, pd):
    barrier = pltpu.get_barrier_semaphore()

    def greet(**where):
        pl.semaphore_signal(barrier, inc=1, device_id=where, device_id_type=MESH)

    for p in (px, py, pd):
        greet(dp=p, feat=f)
    greet(dp=i, feat=f + 1 - 2 * (f % 2))

    @pl.when(z > 0)
    def _():
        greet(dp=i, feat=f - 2)

    @pl.when(z < LINE - 1)
    def _():
        greet(dp=i, feat=f + 2)

    pl.semaphore_wait(barrier, 5 + z * (LINE - 1 - z) // (LINE - 2))


def rcopy(src, dst, send, recv, **where):
    return pltpu.make_async_remote_copy(
        src_ref=src, dst_ref=dst, send_sem=send, recv_sem=recv, device_id=where, device_id_type=MESH
    )


def gather_kernel(
    tokens, cot, inv, weight, tok_all, cot_all, dense, pre, filled, wd, chunk, own, wsem, csem,
    a2a_s, a2a_r, up_s, dn_s, line_r, xy_s, xy_r, dg_s, dg_r, sib_s, sib_r,
):
    i, f, z, c, px, py, pd = place()
    half = tokens.shape[0] // 2
    order = line_order(z)
    sib = f + 1 - 2 * c
    local, slots, units, side = weight.shape
    per = wd.shape[2] // side
    load = pltpu.make_async_copy(weight, filled.at[:, pl.ds(0, slots)], own.at[2])
    load.start()
    filled[:, slots] = jnp.zeros((local, units, side), filled.dtype)
    enter(i, f, z, px, py, pd)

    def owner(q):
        return 2 * order[q // 2] + (c if q % 2 == 0 else 1 - c)

    def keep_dense(q):
        return pltpu.make_async_copy(wd.at[q], dense.at[owner(q)], wsem.at[q])

    def build(q):
        first = owner(q) * per

        def row(r, carry):
            at = pl.ds(pl.multiple_of(r * units, units), units)
            for b in range(per):
                wd[q, at, b * side : (b + 1) * side] = filled[r, inv[r, first + b]]
            return carry

        lax.fori_loop(0, local, row, 0)
        keep_dense(q).start()

    def forward(q):
        fetch = pltpu.make_async_copy(tok_all.at[:, owner(q)], chunk, csem)
        fetch.start()
        fetch.wait()
        pair = 2 * chunk.shape[1]

        def body(n, carry):
            lanes = pl.ds(pl.multiple_of(n * pair, pair), pair)
            x = chunk[pl.ds(2 * n, 2)].reshape(pair, chunk.shape[2])
            res = lax.dot_general(
                wd[q], x, (((1,), (1,)), ((), ())), preferred_element_type=jnp.float32
            )
            pre[:, lanes] = res if q == 0 else pre[:, lanes] + res
            return carry

        lax.fori_loop(0, chunk.shape[0] // 2, body, 0)

    mine = pltpu.make_async_copy(tokens, tok_all.at[i, f], own.at[0])
    mine.start()
    keep = pltpu.make_async_copy(cot.at[i], cot_all.at[i], own.at[1])
    keep.start()

    def blk(who, zp):
        return tok_all.at[who, 2 * zp + c]

    def src(k):
        return tokens if k == 0 else blk(i, order[k])

    def up(k):
        return rcopy(src(k), blk(i, order[k]), up_s.at[k], line_r.at[order[k]], dp=i, feat=f + 2)

    def down(k):
        return rcopy(src(k), blk(i, order[k]), dn_s.at[k], line_r.at[order[k]], dp=i, feat=f - 2)

    def across(k, n):
        return rcopy(
            src(k), blk(i, order[k]), xy_s.at[n, k], xy_r.at[n, k], dp=(px, py)[n], feat=f
        )

    def corner(k, n):
        rows = pl.ds(n * half, half)
        ref = blk((px, py)[n], order[k]).at[rows]
        return rcopy(ref, ref, dg_s.at[n, k], dg_r.at[n, k], dp=(py, px)[n], feat=f)

    def twin(k, w):
        who = (i, px, py, pd)[w]
        ref = blk(who, order[k])
        s = src(k) if w == 0 else ref
        return rcopy(s, ref, sib_s.at[w, k], sib_r.at[w, k], dp=i, feat=sib)

    def exchange(n):
        p = (px, py, pd)[n]
        return rcopy(cot.at[p], cot_all.at[i], a2a_s.at[n], a2a_r.at[n], dp=p, feat=f)

    def goes_up(k):
        return jnp.logical_and(order[k] <= z, z < LINE - 1)

    def goes_down(k):
        return jnp.logical_and(order[k] >= z, z > 0)

    builds = ((0, 1, 2), (3, 4, 5), (6, 7))
    for k in range(LINE + 3):
        if k < LINE:
            if k > 0:
                pltpu.make_async_copy(
                    blk(i, order[k]), blk(i, order[k]), line_r.at[order[k]]
                ).wait()
            pl.when(goes_up(k))(lambda: up(k).start())
            pl.when(goes_down(k))(lambda: down(k).start())
            for n in range(2):
                across(k, n).start()
            twin(k, 0).start()
        if 1 <= k <= LINE:
            for n in range(2):
                across(k - 1, n).wait_recv()
                corner(k - 1, n).start()
                twin(k - 1, 1 + n).start()
        if 2 <= k < LINE + 2:
            for n in range(2):
                corner(k - 2, n).wait_recv()
            twin(k - 2, 3).start()
        if k == 1:
            for n in range(3):
                exchange(n).start()
        if k == 0:
            load.wait()
        if k < len(builds):
            for q in builds[k]:
                build(q)
        if k == 2:
            mine.wait()
        if 2 <= k < LINE + 2:
            forward(2 * (k - 2))
        if k >= 3:
            for w in range(4):
                twin(k - 3, w).wait_recv()
            forward(2 * (k - 3) + 1)

    for n in range(3):
        exchange(n).wait()
    for q in range(2 * LINE):
        keep_dense(q).wait()
    keep.wait()
    for k in range(LINE):
        pl.when(goes_up(k))(lambda: up(k).wait_send())
        pl.when(goes_down(k))(lambda: down(k).wait_send())
        for n in range(2):
            across(k, n).wait_send()
            corner(k, n).wait_send()
        for w in range(4):
            twin(k, w).wait_send()


def local_kernel(cols, tok, pre, cot, hid, wgrad, grad_t, picked):
    step = pl.program_id(0)
    n, slots, units, side = wgrad.shape
    groups, _, rows, wide = tok.shape
    per = wide // side
    grads = []
    for a in range(n):
        for s in range(slots):
            b = cols[step * n + a, s]
            lanes = pl.ds(pl.multiple_of((b % per) * side, side), side)
            for g in range(groups):
                picked[a % 2, g * rows : (g + 1) * rows, s * side : (s + 1) * side] = tok[
                    g, b // per, :, lanes
                ]
        x = picked.at[a % 2]
        v = pre[a * units : (a + 1) * units, :]
        k0, k1 = 0.7978845608028654, 0.044715
        th = jnp.tanh(k0 * (v + k1 * v * v * v))
        act = (0.5 * v * (1.0 + th)).astype(jnp.bfloat16)
        slope = 0.5 * (1.0 + th) + 0.5 * v * (1.0 - th * th) * (k0 * (1.0 + 3.0 * k1 * v * v))
        ct = jnp.concatenate([cot[g, a] for g in range(groups)], axis=1).astype(jnp.float32)
        grad = ct * slope
        grads.append(grad)
        grad = grad.astype(jnp.bfloat16)
        for g in range(groups):
            hid[g, a] = act[:, g * rows : (g + 1) * rows]
        wg = jnp.dot(grad, x[...], preferred_element_type=jnp.float32).astype(jnp.bfloat16)
        for s in range(slots):
            wgrad[a, s] = wg[:, s * side : (s + 1) * side]
    grad_t[...] = jnp.concatenate(grads, axis=0).T.astype(jnp.bfloat16)


def scatter_kernel(
    grad_t, wd, hid, out, hid_all, wbuf, part, sibbuf, xhalf, yhalf, xfull, yfull, upbuf, dnbuf,
    own, wsem, a2a_s, a2a_r, sib_s, sib_r, half_s, half_r, full_s, full_r, up_s, up_r, dn_s, dn_r,
):
    i, f, z, c, px, py, pd = place()
    groups, rows, wide = sibbuf.shape[1:]
    half = rows // 2
    order = line_order(z)[::-1]
    sib = f + 1 - 2 * c
    tile = 256

    def fetch(q):
        k, own_side = q // 2, q % 2
        col = 2 * order[k] + (c if own_side else 1 - c)
        return pltpu.make_async_copy(wd.at[col], wbuf.at[q % 2], wsem.at[q % 2])

    fetch(0).start()
    enter(i, f, z, px, py, pd)
    keep = pltpu.make_async_copy(hid.at[i], hid_all.at[i], own)
    keep.start()

    def exchange(n):
        p = (px, py, pd)[n]
        return rcopy(hid.at[p], hid_all.at[i], a2a_s.at[n], a2a_r.at[n], dp=p, feat=f)

    def work(q):
        k = q // 2
        fetch(q).wait()
        if q + 1 < 2 * LINE:
            fetch(q + 1).start()

        def body(n, carry):
            lanes = pl.ds(pl.multiple_of(n * tile, tile), tile)
            res = jnp.dot(
                grad_t[...], wbuf[q % 2, :, lanes], preferred_element_type=jnp.float32
            ).astype(jnp.bfloat16)
            for g in range(groups):
                part[q % 2, k, g, :, lanes] = res[g * rows : (g + 1) * rows]
            return carry

        lax.fori_loop(0, wide // tile, body, 0)

    def add(dst, *others):
        def body(n, carry):
            at = pl.ds(pl.multiple_of(n * 16, 16), 16)
            total = dst[at].astype(jnp.float32)
            for o in others:
                total = total + o[at].astype(jnp.float32)
            dst[at] = total.astype(jnp.bfloat16)
            return carry

        lax.fori_loop(0, dst.shape[0] // 16, body, 0)

    def twin(k):
        return rcopy(part.at[0, k], sibbuf.at[k], sib_s.at[k], sib_r.at[k], dp=i, feat=sib)

    first, second = pl.ds(0, half), pl.ds(half, half)

    def corner(k, n):
        rows_n = (first, second)[n]
        return rcopy(
            part.at[1, k, pd, rows_n], (xhalf, yhalf)[n].at[k], half_s.at[n, k], half_r.at[n, k],
            dp=(px, py)[n], feat=f,
        )

    def across(k, n):
        p = (px, py)[n]
        return rcopy(
            part.at[1, k, p], (xfull, yfull)[n].at[k], full_s.at[n, k], full_r.at[n, k],
            dp=p, feat=f,
        )

    def up(k):
        return rcopy(
            part.at[1, k, i], upbuf.at[order[k]], up_s.at[k], up_r.at[order[k]], dp=i, feat=f + 2
        )

    def down(k):
        return rcopy(
            part.at[1, k, i], dnbuf.at[order[k]], dn_s.at[k], dn_r.at[order[k]], dp=i, feat=f - 2
        )

    def got(buf, sem, k):
        ref = buf.at[order[k]]
        pltpu.make_async_copy(ref, ref, sem.at[order[k]]).wait()

    def from_below(k):
        return jnp.logical_and(order[k] >= z, z > 0)

    def from_above(k):
        return jnp.logical_and(order[k] <= z, z < LINE - 1)

    for step in range(LINE + 3):
        k = step
        if k < LINE:
            work(2 * k)
            twin(k).start()
            work(2 * k + 1)
            if k == 0:
                for n in range(3):
                    exchange(n).start()
            twin(k).wait_recv()
            for g in (pd, px, py, i):
                add(part.at[1, k, g], sibbuf.at[k, g])
                if g is pd:
                    corner(k, 0).start()
                    corner(k, 1).start()
        k = step - 1
        if 0 <= k < LINE:
            corner(k, 0).wait_recv()
            add(part.at[1, k, py, first], xhalf.at[k])
            across(k, 1).start()
            corner(k, 1).wait_recv()
            add(part.at[1, k, px, second], yhalf.at[k])
            across(k, 0).start()
        k = step - 2
        if 0 <= k < LINE:
            across(k, 0).wait_recv()
            across(k, 1).wait_recv()
            add(part.at[1, k, i], xfull.at[k], yfull.at[k])
        k = step - 3
        if 0 <= k < LINE:
            mine = part.at[1, k, i]

            @pl.when(from_below(k))
            def _():
                got(upbuf, up_r, k)
                add(mine, upbuf.at[order[k]])

            @pl.when(from_above(k))
            def _():
                got(dnbuf, dn_r, k)
                add(mine, dnbuf.at[order[k]])

            if k < LINE - 1:
                pl.when(order[k] > z)(lambda: up(k).start())
                pl.when(order[k] < z)(lambda: down(k).start())

    done = pltpu.make_async_copy(part.at[1, LINE - 1, i], out, wsem.at[0])
    done.start()
    for n in range(3):
        exchange(n).wait()
    keep.wait()
    for k in range(LINE):
        twin(k).wait_send()
        for n in range(2):
            corner(k, n).wait_send()
            across(k, n).wait_send()
        if k < LINE - 1:
            pl.when(order[k] > z)(lambda: up(k).wait_send())
            pl.when(order[k] < z)(lambda: down(k).wait_send())
    done.wait()


def token_plan(tokens, columns, weight, cotangent):
    rows, wide = tokens.shape
    local, slots, units, side = weight.shape
    n_dp, n_feat = lax.axis_size("dp"), lax.axis_size("feat")
    bf = jnp.bfloat16
    dma = pltpu.SemaphoreType.DMA
    anywhere = pl.BlockSpec(memory_space=pl.ANY)
    inside = pl.BlockSpec(memory_space=pltpu.VMEM)
    blocks = n_feat * wide // side
    total = n_dp * rows

    cot_t = cotangent.reshape(rows, local, n_dp, units).transpose(2, 1, 3, 0)
    hit = columns[:, :, None] == jnp.arange(blocks, dtype=jnp.int32)
    inv = jnp.min(jnp.where(hit, jnp.arange(slots, dtype=jnp.int32)[:, None], slots), axis=1)
    tok_all, cot_all, dense, pre = pl.pallas_call(
        gather_kernel,
        out_shape=(
            jax.ShapeDtypeStruct((n_dp, n_feat, rows, wide), bf),
            jax.ShapeDtypeStruct(cot_t.shape, bf),
            jax.ShapeDtypeStruct((n_feat, local * units, wide), bf),
            jax.ShapeDtypeStruct((local * units, total), jnp.float32),
        ),
        in_specs=[anywhere, anywhere, pl.BlockSpec(memory_space=pltpu.SMEM), anywhere],
        out_specs=(anywhere, anywhere, anywhere, inside),
        scratch_shapes=[
            pltpu.VMEM((local, slots + 1, units, side), bf),
            pltpu.VMEM((n_feat, local * units, wide), bf),
            pltpu.VMEM((n_dp, rows, wide), bf),
            dma((3,)), dma((n_feat,)), dma(()),
            dma((3,)), dma((3,)), dma((LINE,)), dma((LINE,)), dma((LINE,)),
            dma((2, LINE)), dma((2, LINE)), dma((2, LINE)), dma((2, LINE)),
            dma((4, LINE)), dma((4, LINE)),
        ],
        compiler_params=pltpu.CompilerParams(
            collective_id=0, has_side_effects=True, vmem_limit_bytes=56 * 2**20
        ),
        name="gather",
    )(tokens, cot_t, inv, weight)

    n = side // units
    hid_t, weight_grad, grad_t = pl.pallas_call(
        local_kernel,
        out_shape=(
            jax.ShapeDtypeStruct(cot_t.shape, bf),
            jax.ShapeDtypeStruct(weight.shape, bf),
            jax.ShapeDtypeStruct((total, local * units), bf),
        ),
        grid_spec=pltpu.PrefetchScalarGridSpec(
            num_scalar_prefetch=1,
            grid=(local // n,),
            in_specs=[
                inside,
                pl.BlockSpec((n * units, total), lambda r, c: (r, 0)),
                pl.BlockSpec((n_dp, n, units, rows), lambda r, c: (0, r, 0, 0)),
            ],
            out_specs=(
                pl.BlockSpec((n_dp, n, units, rows), lambda r, c: (0, r, 0, 0)),
                pl.BlockSpec((n, slots, units, side), lambda r, c: (r, 0, 0, 0)),
                pl.BlockSpec((total, n * units), lambda r, c: (0, r)),
            ),
            scratch_shapes=[pltpu.VMEM((2, total, slots * side), bf)],
        ),
        compiler_params=pltpu.CompilerParams(vmem_limit_bytes=48 * 2**20),
        name="local",
    )(columns, tok_all, pre, cot_all)

    input_grad, hid_all = pl.pallas_call(
        scatter_kernel,
        out_shape=(
            jax.ShapeDtypeStruct((rows, wide), bf),
            jax.ShapeDtypeStruct(cot_t.shape, bf),
        ),
        in_specs=[inside, anywhere, anywhere],
        out_specs=(anywhere,) * 2,
        scratch_shapes=[
            pltpu.VMEM((2, local * units, wide), bf),
            pltpu.VMEM((2, LINE, n_dp, rows, wide), bf),
            pltpu.VMEM((LINE, n_dp, rows, wide), bf),
            pltpu.VMEM((LINE, rows // 2, wide), bf),
            pltpu.VMEM((LINE, rows // 2, wide), bf),
            pltpu.VMEM((LINE, rows, wide), bf),
            pltpu.VMEM((LINE, rows, wide), bf),
            pltpu.VMEM((LINE, rows, wide), bf),
            pltpu.VMEM((LINE, rows, wide), bf),
            dma(()), dma((2,)), dma((3,)), dma((3,)), dma((LINE,)), dma((LINE,)),
            dma((2, LINE)), dma((2, LINE)), dma((2, LINE)), dma((2, LINE)),
            dma((LINE,)), dma((LINE,)), dma((LINE,)), dma((LINE,)),
        ],
        compiler_params=pltpu.CompilerParams(
            collective_id=1, has_side_effects=True, vmem_limit_bytes=56 * 2**20
        ),
        name="scatter",
    )(grad_t, dense, hid_t)
    hidden = hid_all.transpose(3, 1, 0, 2).reshape(rows, local * side)
    return (hidden, input_grad, weight_grad)


def solution(mesh):
    in_specs = (P("dp", "feat"), P("feat", None), P("feat", None, "dp", None), P("dp", "feat"))
    out_specs = (P("dp", "feat"), P("dp", "feat"), P("feat", None, "dp", None))
    square = mesh.shape["dp"] == 4 and mesh.shape["feat"] == 2 * LINE
    return jax.shard_map(
        token_plan if square else on_device,
        mesh=mesh, in_specs=in_specs, out_specs=out_specs, check_vma=False,
    )
```

```python
import functools

import jax
import jax.numpy as jnp
from jax import lax
from jax.experimental import pallas as pl
from jax.experimental.pallas import tpu as pltpu
from jax.sharding import PartitionSpec as P

MESH = pl.DeviceIdType.MESH
LINE = 4


def gelu_tanh(value):
    return jax.nn.gelu(value, approximate=True)


def on_device(tokens, columns, weight, cotangent):
    tok_rows = tokens.shape[0]
    local_rows = weight.shape[0]
    slots = weight.shape[1]
    side = weight.shape[3]
    feat_count = lax.axis_size("feat")
    gathered = lax.all_gather(tokens, "feat", axis=1, tiled=True)
    block_count = gathered.shape[1] // side
    flat_cols = columns.reshape(-1)
    picked = gathered.reshape(tok_rows, block_count, side)[:, flat_cols, :].reshape(
        tok_rows, local_rows, slots, side
    )
    full_weight = lax.all_gather(weight, "dp", axis=2, tiled=True)
    pre = jnp.einsum("trsk,rsuk->tru", picked, full_weight, preferred_element_type=jnp.float32)
    act, pull = jax.vjp(gelu_tanh, pre)
    hidden = act.astype(jnp.bfloat16).reshape(tok_rows, local_rows * side)
    grad_pre = pull(cotangent.reshape(tok_rows, local_rows, side).astype(jnp.float32))[0].astype(
        jnp.bfloat16
    )
    weight_terms = jnp.einsum(
        "tru,trsk->rsuk", grad_pre, picked, preferred_element_type=jnp.float32
    )
    weight_grad = lax.psum_scatter(
        weight_terms.astype(jnp.bfloat16), "dp", scatter_dimension=2, tiled=True
    )
    partial_grad = jnp.einsum(
        "tru,rsuk->trsk", grad_pre, full_weight, preferred_element_type=jnp.float32
    )
    onehot = (flat_cols[:, None] == jnp.arange(block_count, dtype=jnp.int32)[None, :]).astype(
        jnp.float32
    )
    spread = jnp.einsum(
        "tqk,qb->tbk",
        partial_grad.reshape(tok_rows, local_rows * slots, side),
        onehot,
        precision=lax.Precision.HIGHEST,
    )
    outgoing = spread.reshape(tok_rows, block_count * side).astype(jnp.bfloat16)
    returned = lax.all_to_all(outgoing, "feat", split_axis=1, concat_axis=0, tiled=True)
    input_grad = jnp.sum(
        returned.reshape(feat_count, tok_rows, -1).astype(jnp.float32), axis=0
    ).astype(jnp.bfloat16)
    return (hidden, input_grad, weight_grad)


def place():
    i, f = lax.axis_index("dp"), lax.axis_index("feat")
    z, c = f // 2, f % 2
    px = i + 1 - 2 * (i % 2)
    py = i + 2 - 4 * (i // 2)
    return i, f, z, c, px, py, 3 - i


def line_order(z):
    m = z // 2
    zz = z + m * (3 - 2 * z)
    near = [zz, 1 - zz, 2 + 0 * zz, 3 + 0 * zz]
    return [q + m * (3 - 2 * q) for q in near]


def enter(i, f, z, px, py, pd):
    barrier = pltpu.get_barrier_semaphore()

    def greet(**where):
        pl.semaphore_signal(barrier, inc=1, device_id=where, device_id_type=MESH)

    for p in (px, py, pd):
        greet(dp=p, feat=f)
    greet(dp=i, feat=f + 1 - 2 * (f % 2))

    @pl.when(z > 0)
    def _():
        greet(dp=i, feat=f - 2)

    @pl.when(z < LINE - 1)
    def _():
        greet(dp=i, feat=f + 2)

    pl.semaphore_wait(barrier, 5 + z * (LINE - 1 - z) // (LINE - 2))


def rcopy(src, dst, send, recv, **where):
    return pltpu.make_async_remote_copy(
        src_ref=src, dst_ref=dst, send_sem=send, recv_sem=recv, device_id=where, device_id_type=MESH
    )


def gather_kernel(
    tokens, cot, inv, weight, tok_all, cot_all, dense, pre, filled, wd, chunk, own, wsem, csem,
    a2a_s, a2a_r, up_s, dn_s, line_r, up2_s, dn2_s, line2_r, xy_s, xy_r, dg_s, dg_r, sib_s, sib_r,
):
    i, f, z, c, px, py, pd = place()
    half = tokens.shape[0] // 2
    order = line_order(z)
    sib = f + 1 - 2 * c
    local, slots, units, side = weight.shape
    per = wd.shape[2] // side
    load = pltpu.make_async_copy(weight, filled.at[:, pl.ds(0, slots)], own.at[2])
    load.start()
    filled[:, slots] = jnp.zeros((local, units, side), filled.dtype)
    enter(i, f, z, px, py, pd)

    def owner(q):
        return 2 * order[q // 2] + (c if q % 2 == 0 else 1 - c)

    def keep_dense(q):
        return pltpu.make_async_copy(wd.at[q], dense.at[owner(q)], wsem.at[q])

    def build(q):
        first = owner(q) * per

        def row(r, carry):
            at = pl.ds(pl.multiple_of(r * units, units), units)
            for b in range(per):
                wd[q, at, b * side : (b + 1) * side] = filled[r, inv[r, first + b]]
            return carry

        lax.fori_loop(0, local, row, 0)
        keep_dense(q).start()

    def forward(q):
        fetch = pltpu.make_async_copy(tok_all.at[:, owner(q)], chunk, csem)
        fetch.start()
        fetch.wait()
        pair = 2 * chunk.shape[1]

        def body(n, carry):
            lanes = pl.ds(pl.multiple_of(n * pair, pair), pair)
            x = chunk[pl.ds(2 * n, 2)].reshape(pair, chunk.shape[2])
            res = lax.dot_general(
                wd[q], x, (((1,), (1,)), ((), ())), preferred_element_type=jnp.float32
            )
            pre[:, lanes] = res if q == 0 else pre[:, lanes] + res
            return carry

        lax.fori_loop(0, chunk.shape[0] // 2, body, 0)

    mine = pltpu.make_async_copy(tokens, tok_all.at[i, f], own.at[0])
    mine.start()
    keep = pltpu.make_async_copy(cot.at[i], cot_all.at[i], own.at[1])
    keep.start()

    def blk(who, zp):
        return tok_all.at[who, 2 * zp + c]

    def src(k):
        return tokens if k == 0 else blk(i, order[k])

    def up(k):
        return rcopy(src(k), blk(i, order[k]), up_s.at[k], line_r.at[order[k]], dp=i, feat=f + 2)

    def down(k):
        return rcopy(src(k), blk(i, order[k]), dn_s.at[k], line_r.at[order[k]], dp=i, feat=f - 2)

    def up2(k):
        ref = blk(pd, order[k])
        return rcopy(ref, ref, up2_s.at[k], line2_r.at[order[k]], dp=i, feat=f + 2)

    def down2(k):
        ref = blk(pd, order[k])
        return rcopy(ref, ref, dn2_s.at[k], line2_r.at[order[k]], dp=i, feat=f - 2)

    def across(k, n):
        return rcopy(
            src(k), blk(i, order[k]), xy_s.at[n, k], xy_r.at[n, k], dp=(px, py)[n], feat=f
        )

    def corner(k, n):
        rows = pl.ds(n * half, half)
        ref = blk((px, py)[n], order[k]).at[rows]
        return rcopy(ref, ref, dg_s.at[n], dg_r.at[n], dp=(py, px)[n], feat=f)

    def twin(k, w):
        who = (i, px, py, pd)[w]
        ref = blk(who, order[k])
        s = src(k) if w == 0 else ref
        return rcopy(s, ref, sib_s.at[w, k], sib_r.at[w, k], dp=i, feat=sib)

    def exchange(n):
        p = (px, py, pd)[n]
        return rcopy(cot.at[p], cot_all.at[i], a2a_s.at[n], a2a_r.at[n], dp=p, feat=f)

    def goes_up(k):
        return jnp.logical_and(order[k] <= z, z < LINE - 1)

    def goes_down(k):
        return jnp.logical_and(order[k] >= z, z > 0)

    builds = ((0, 1, 2), (3, 4, 5), (6, 7))
    for k in range(LINE + 3):
        if k < LINE:
            if k > 0:
                pltpu.make_async_copy(
                    blk(i, order[k]), blk(i, order[k]), line_r.at[order[k]]
                ).wait()
            pl.when(goes_up(k))(lambda: up(k).start())
            pl.when(goes_down(k))(lambda: down(k).start())
            for n in range(2):
                across(k, n).start()
            twin(k, 0).start()
        if 1 <= k <= LINE:
            for n in range(2):
                across(k - 1, n).wait_recv()
                if k == 1:
                    corner(0, n).start()
                twin(k - 1, 1 + n).start()
        if 2 <= k < LINE + 2:
            if k == 2:
                for n in range(2):
                    corner(0, n).wait_recv()
            else:
                ref = blk(pd, order[k - 2])
                pltpu.make_async_copy(ref, ref, line2_r.at[order[k - 2]]).wait()
            pl.when(goes_up(k - 2))(lambda: up2(k - 2).start())
            pl.when(goes_down(k - 2))(lambda: down2(k - 2).start())
            twin(k - 2, 3).start()
        if k == 1:
            for n in range(3):
                exchange(n).start()
        if k == 0:
            load.wait()
        if k < len(builds):
            for q in builds[k]:
                build(q)
        if k == 2:
            mine.wait()
        if 2 <= k < LINE + 2:
            forward(2 * (k - 2))
        if k >= 3:
            for w in range(4):
                twin(k - 3, w).wait_recv()
            forward(2 * (k - 3) + 1)

    for n in range(3):
        exchange(n).wait()
    for q in range(2 * LINE):
        keep_dense(q).wait()
    keep.wait()
    for k in range(LINE):
        pl.when(goes_up(k))(lambda: up(k).wait_send())
        pl.when(goes_down(k))(lambda: down(k).wait_send())
        pl.when(goes_up(k))(lambda: up2(k).wait_send())
        pl.when(goes_down(k))(lambda: down2(k).wait_send())
        for n in range(2):
            across(k, n).wait_send()
            if k == 0:
                corner(k, n).wait_send()
        for w in range(4):
            twin(k, w).wait_send()


def local_kernel(cols, tok, pre, cot, hid, wgrad, grad_t, picked):
    step = pl.program_id(0)
    n, slots, units, side = wgrad.shape
    groups, _, rows, wide = tok.shape
    per = wide // side
    grads = []
    for a in range(n):
        for s in range(slots):
            b = cols[step * n + a, s]
            lanes = pl.ds(pl.multiple_of((b % per) * side, side), side)
            for g in range(groups):
                picked[a % 2, g * rows : (g + 1) * rows, s * side : (s + 1) * side] = tok[
                    g, b // per, :, lanes
                ]
        x = picked.at[a % 2]
        v = pre[a * units : (a + 1) * units, :]
        k0, k1 = 0.7978845608028654, 0.044715
        th = jnp.tanh(k0 * (v + k1 * v * v * v))
        act = (0.5 * v * (1.0 + th)).astype(jnp.bfloat16)
        slope = 0.5 * (1.0 + th) + 0.5 * v * (1.0 - th * th) * (k0 * (1.0 + 3.0 * k1 * v * v))
        ct = jnp.concatenate([cot[g, a] for g in range(groups)], axis=1).astype(jnp.float32)
        grad = ct * slope
        grads.append(grad)
        grad = grad.astype(jnp.bfloat16)
        for g in range(groups):
            hid[g, a] = act[:, g * rows : (g + 1) * rows]
        wg = jnp.dot(grad, x[...], preferred_element_type=jnp.float32).astype(jnp.bfloat16)
        for s in range(slots):
            wgrad[a, s] = wg[:, s * side : (s + 1) * side]
    grad_t[...] = jnp.concatenate(grads, axis=0).T.astype(jnp.bfloat16)


def scatter_kernel(
    grad_t, wd, hid, out, hid_all, wbuf, part, sibbuf, xhalf, yhalf, xfull, yfull, upbuf, dnbuf,
    up2buf, dn2buf, own, wsem, a2a_s, a2a_r, sib_s, sib_r, half_s, half_r, full_s, full_r, up_s, up_r, dn_s, dn_r,
    up2_s, up2_r, dn2_s, dn2_r,
):
    i, f, z, c, px, py, pd = place()
    groups, rows, wide = sibbuf.shape[1:]
    half = rows // 2
    order = line_order(z)[::-1]
    sib = f + 1 - 2 * c
    tile = 256

    def fetch(q):
        k, own_side = q // 2, q % 2
        col = 2 * order[k] + (c if own_side else 1 - c)
        return pltpu.make_async_copy(wd.at[col], wbuf.at[q % 2], wsem.at[q % 2])

    fetch(0).start()
    enter(i, f, z, px, py, pd)
    keep = pltpu.make_async_copy(hid.at[i], hid_all.at[i], own)
    keep.start()

    def exchange(n):
        p = (px, py, pd)[n]
        return rcopy(hid.at[p], hid_all.at[i], a2a_s.at[n], a2a_r.at[n], dp=p, feat=f)

    def work(q):
        k = q // 2
        fetch(q).wait()
        if q + 1 < 2 * LINE:
            fetch(q + 1).start()

        def body(n, carry):
            lanes = pl.ds(pl.multiple_of(n * tile, tile), tile)
            res = jnp.dot(
                grad_t[...], wbuf[q % 2, :, lanes], preferred_element_type=jnp.float32
            ).astype(jnp.bfloat16)
            for g in range(groups):
                part[q % 2, k, g, :, lanes] = res[g * rows : (g + 1) * rows]
            return carry

        lax.fori_loop(0, wide // tile, body, 0)

    def add(dst, *others):
        def body(n, carry):
            at = pl.ds(pl.multiple_of(n * 16, 16), 16)
            total = dst[at].astype(jnp.float32)
            for o in others:
                total = total + o[at].astype(jnp.float32)
            dst[at] = total.astype(jnp.bfloat16)
            return carry

        lax.fori_loop(0, dst.shape[0] // 16, body, 0)

    def twin(k):
        return rcopy(part.at[0, k], sibbuf.at[k], sib_s.at[k], sib_r.at[k], dp=i, feat=sib)

    first, second = pl.ds(0, half), pl.ds(half, half)

    def corner(k, n):
        rows_n = (first, second)[n]
        return rcopy(
            part.at[1, k, pd, rows_n], (xhalf, yhalf)[n], half_s.at[n], half_r.at[n],
            dp=(px, py)[n], feat=f,
        )

    def across(k, n):
        p = (px, py)[n]
        return rcopy(
            part.at[1, k, p], (xfull, yfull)[n].at[k], full_s.at[n, k], full_r.at[n, k],
            dp=p, feat=f,
        )

    def up(k):
        return rcopy(
            part.at[1, k, i], upbuf.at[order[k]], up_s.at[k], up_r.at[order[k]], dp=i, feat=f + 2
        )

    def down(k):
        return rcopy(
            part.at[1, k, i], dnbuf.at[order[k]], dn_s.at[k], dn_r.at[order[k]], dp=i, feat=f - 2
        )

    def up2(k):
        return rcopy(
            part.at[1, k, pd], up2buf.at[order[k]], up2_s.at[k], up2_r.at[order[k]], dp=i, feat=f + 2
        )

    def down2(k):
        return rcopy(
            part.at[1, k, pd], dn2buf.at[order[k]], dn2_s.at[k], dn2_r.at[order[k]], dp=i, feat=f - 2
        )

    def got(buf, sem, k):
        ref = buf.at[order[k]]
        pltpu.make_async_copy(ref, ref, sem.at[order[k]]).wait()

    def from_below(k):
        return jnp.logical_and(order[k] >= z, z > 0)

    def from_above(k):
        return jnp.logical_and(order[k] <= z, z < LINE - 1)

    def collect(k, mine, ups, downs):
        @pl.when(from_below(k))
        def _():
            got(ups[0], ups[1], k)
            add(mine, ups[0].at[order[k]])

        @pl.when(from_above(k))
        def _():
            got(downs[0], downs[1], k)
            add(mine, downs[0].at[order[k]])

    last = LINE - 1
    for step in range(LINE + 2):
        k = step
        if k < LINE:
            work(2 * k)
            twin(k).start()
            work(2 * k + 1)
            if k == 0:
                for n in range(3):
                    exchange(n).start()
            twin(k).wait_recv()
            add(part.at[1, k, pd], sibbuf.at[k, pd])
            for n, g in ((0, px), (1, py)):
                add(part.at[1, k, g], sibbuf.at[k, g])
                if k < last:
                    across(k, n).start()
            add(part.at[1, k, i], sibbuf.at[k, i])
            collect(k, part.at[1, k, pd], (up2buf, up2_r), (dn2buf, dn2_r))
            if k < last:
                pl.when(order[k] > z)(lambda: up2(k).start())
                pl.when(order[k] < z)(lambda: down2(k).start())
            else:
                corner(k, 0).start()
                corner(k, 1).start()
        k = step - 1
        if 0 <= k < LINE:
            if k == last:
                corner(k, 0).wait_recv()
                add(part.at[1, k, py, first], xhalf)
                across(k, 1).start()
                corner(k, 1).wait_recv()
                add(part.at[1, k, px, second], yhalf)
                across(k, 0).start()
            else:
                across(k, 0).wait_recv()
                across(k, 1).wait_recv()
                add(part.at[1, k, i], xfull.at[k], yfull.at[k])
                collect(k, part.at[1, k, i], (upbuf, up_r), (dnbuf, dn_r))
                pl.when(order[k] > z)(lambda: up(k).start())
                pl.when(order[k] < z)(lambda: down(k).start())
        if step == LINE + 1:
            collect(last, part.at[1, last, i], (upbuf, up_r), (dnbuf, dn_r))
            across(last, 0).wait_recv()
            across(last, 1).wait_recv()
            add(part.at[1, last, i], xfull.at[last], yfull.at[last])

    done = pltpu.make_async_copy(part.at[1, LINE - 1, i], out, wsem.at[0])
    done.start()
    for n in range(3):
        exchange(n).wait()
    keep.wait()
    for k in range(LINE):
        twin(k).wait_send()
        for n in range(2):
            if k == last:
                corner(k, n).wait_send()
            across(k, n).wait_send()
        if k < last:
            pl.when(order[k] > z)(lambda: up(k).wait_send())
            pl.when(order[k] < z)(lambda: down(k).wait_send())
            pl.when(order[k] > z)(lambda: up2(k).wait_send())
            pl.when(order[k] < z)(lambda: down2(k).wait_send())
    done.wait()


def token_plan(tokens, columns, weight, cotangent):
    rows, wide = tokens.shape
    local, slots, units, side = weight.shape
    n_dp, n_feat = lax.axis_size("dp"), lax.axis_size("feat")
    bf = jnp.bfloat16
    dma = pltpu.SemaphoreType.DMA
    anywhere = pl.BlockSpec(memory_space=pl.ANY)
    inside = pl.BlockSpec(memory_space=pltpu.VMEM)
    blocks = n_feat * wide // side
    total = n_dp * rows

    cot_t = cotangent.reshape(rows, local, n_dp, units).transpose(2, 1, 3, 0)
    hit = columns[:, :, None] == jnp.arange(blocks, dtype=jnp.int32)
    inv = jnp.min(jnp.where(hit, jnp.arange(slots, dtype=jnp.int32)[:, None], slots), axis=1)
    tok_all, cot_all, dense, pre = pl.pallas_call(
        gather_kernel,
        out_shape=(
            jax.ShapeDtypeStruct((n_dp, n_feat, rows, wide), bf),
            jax.ShapeDtypeStruct(cot_t.shape, bf),
            jax.ShapeDtypeStruct((n_feat, local * units, wide), bf),
            jax.ShapeDtypeStruct((local * units, total), jnp.float32),
        ),
        in_specs=[anywhere, anywhere, pl.BlockSpec(memory_space=pltpu.SMEM), anywhere],
        out_specs=(anywhere, anywhere, anywhere, inside),
        scratch_shapes=[
            pltpu.VMEM((local, slots + 1, units, side), bf),
            pltpu.VMEM((n_feat, local * units, wide), bf),
            pltpu.VMEM((n_dp, rows, wide), bf),
            dma((3,)), dma((n_feat,)), dma(()),
            dma((3,)), dma((3,)), dma((LINE,)), dma((LINE,)), dma((LINE,)),
            dma((LINE,)), dma((LINE,)), dma((LINE,)),
            dma((2, LINE)), dma((2, LINE)), dma((2,)), dma((2,)),
            dma((4, LINE)), dma((4, LINE)),
        ],
        compiler_params=pltpu.CompilerParams(
            collective_id=0, has_side_effects=True, vmem_limit_bytes=56 * 2**20
        ),
        name="gather",
    )(tokens, cot_t, inv, weight)

    n = side // units
    hid_t, weight_grad, grad_t = pl.pallas_call(
        local_kernel,
        out_shape=(
            jax.ShapeDtypeStruct(cot_t.shape, bf),
            jax.ShapeDtypeStruct(weight.shape, bf),
            jax.ShapeDtypeStruct((total, local * units), bf),
        ),
        grid_spec=pltpu.PrefetchScalarGridSpec(
            num_scalar_prefetch=1,
            grid=(local // n,),
            in_specs=[
                inside,
                pl.BlockSpec((n * units, total), lambda r, c: (r, 0)),
                pl.BlockSpec((n_dp, n, units, rows), lambda r, c: (0, r, 0, 0)),
            ],
            out_specs=(
                pl.BlockSpec((n_dp, n, units, rows), lambda r, c: (0, r, 0, 0)),
                pl.BlockSpec((n, slots, units, side), lambda r, c: (r, 0, 0, 0)),
                pl.BlockSpec((total, n * units), lambda r, c: (0, r)),
            ),
            scratch_shapes=[pltpu.VMEM((2, total, slots * side), bf)],
        ),
        compiler_params=pltpu.CompilerParams(vmem_limit_bytes=48 * 2**20),
        name="local",
    )(columns, tok_all, pre, cot_all)

    input_grad, hid_all = pl.pallas_call(
        scatter_kernel,
        out_shape=(
            jax.ShapeDtypeStruct((rows, wide), bf),
            jax.ShapeDtypeStruct(cot_t.shape, bf),
        ),
        in_specs=[inside, anywhere, anywhere],
        out_specs=(anywhere,) * 2,
        scratch_shapes=[
            pltpu.VMEM((2, local * units, wide), bf),
            pltpu.VMEM((2, LINE, n_dp, rows, wide), bf),
            pltpu.VMEM((LINE, n_dp, rows, wide), bf),
            pltpu.VMEM((rows // 2, wide), bf),
            pltpu.VMEM((rows // 2, wide), bf),
            pltpu.VMEM((LINE, rows, wide), bf),
            pltpu.VMEM((LINE, rows, wide), bf),
            pltpu.VMEM((LINE, rows, wide), bf),
            pltpu.VMEM((LINE, rows, wide), bf),
            pltpu.VMEM((LINE, rows, wide), bf),
            pltpu.VMEM((LINE, rows, wide), bf),
            dma(()), dma((2,)), dma((3,)), dma((3,)), dma((LINE,)), dma((LINE,)),
            dma((2,)), dma((2,)), dma((2, LINE)), dma((2, LINE)),
            dma((LINE,)), dma((LINE,)), dma((LINE,)), dma((LINE,)),
            dma((LINE,)), dma((LINE,)), dma((LINE,)), dma((LINE,)),
        ],
        compiler_params=pltpu.CompilerParams(
            collective_id=1, has_side_effects=True, vmem_limit_bytes=56 * 2**20
        ),
        name="scatter",
    )(grad_t, dense, hid_t)
    hidden = hid_all.transpose(3, 1, 0, 2).reshape(rows, local * side)
    return (hidden, input_grad, weight_grad)


def solution(mesh):
    in_specs = (P("dp", "feat"), P("feat", None), P("feat", None, "dp", None), P("dp", "feat"))
    out_specs = (P("dp", "feat"), P("dp", "feat"), P("feat", None, "dp", None))
    square = mesh.shape["dp"] == 4 and mesh.shape["feat"] == 2 * LINE
    return jax.shard_map(
        token_plan if square else on_device,
        mesh=mesh, in_specs=in_specs, out_specs=out_specs, check_vma=False,
    )
```

```python
import functools

import jax
import jax.numpy as jnp
from jax import lax
from jax.experimental import pallas as pl
from jax.experimental.pallas import tpu as pltpu
from jax.sharding import PartitionSpec as P

MESH = pl.DeviceIdType.MESH
LINE = 4


def gelu_tanh(value):
    return jax.nn.gelu(value, approximate=True)


def on_device(tokens, columns, weight, cotangent):
    tok_rows = tokens.shape[0]
    local_rows = weight.shape[0]
    slots = weight.shape[1]
    side = weight.shape[3]
    feat_count = lax.axis_size("feat")
    gathered = lax.all_gather(tokens, "feat", axis=1, tiled=True)
    block_count = gathered.shape[1] // side
    flat_cols = columns.reshape(-1)
    picked = gathered.reshape(tok_rows, block_count, side)[:, flat_cols, :].reshape(
        tok_rows, local_rows, slots, side
    )
    full_weight = lax.all_gather(weight, "dp", axis=2, tiled=True)
    pre = jnp.einsum("trsk,rsuk->tru", picked, full_weight, preferred_element_type=jnp.float32)
    act, pull = jax.vjp(gelu_tanh, pre)
    hidden = act.astype(jnp.bfloat16).reshape(tok_rows, local_rows * side)
    grad_pre = pull(cotangent.reshape(tok_rows, local_rows, side).astype(jnp.float32))[0].astype(
        jnp.bfloat16
    )
    weight_terms = jnp.einsum(
        "tru,trsk->rsuk", grad_pre, picked, preferred_element_type=jnp.float32
    )
    weight_grad = lax.psum_scatter(
        weight_terms.astype(jnp.bfloat16), "dp", scatter_dimension=2, tiled=True
    )
    partial_grad = jnp.einsum(
        "tru,rsuk->trsk", grad_pre, full_weight, preferred_element_type=jnp.float32
    )
    onehot = (flat_cols[:, None] == jnp.arange(block_count, dtype=jnp.int32)[None, :]).astype(
        jnp.float32
    )
    spread = jnp.einsum(
        "tqk,qb->tbk",
        partial_grad.reshape(tok_rows, local_rows * slots, side),
        onehot,
        precision=lax.Precision.HIGHEST,
    )
    outgoing = spread.reshape(tok_rows, block_count * side).astype(jnp.bfloat16)
    returned = lax.all_to_all(outgoing, "feat", split_axis=1, concat_axis=0, tiled=True)
    input_grad = jnp.sum(
        returned.reshape(feat_count, tok_rows, -1).astype(jnp.float32), axis=0
    ).astype(jnp.bfloat16)
    return (hidden, input_grad, weight_grad)


def place():
    i, f = lax.axis_index("dp"), lax.axis_index("feat")
    z, c = f // 2, f % 2
    px = i + 1 - 2 * (i % 2)
    py = i + 2 - 4 * (i // 2)
    return i, f, z, c, px, py, 3 - i


def line_order(z):
    m = z // 2
    zz = z + m * (3 - 2 * z)
    near = [zz, 1 - zz, 2 + 0 * zz, 3 + 0 * zz]
    return [q + m * (3 - 2 * q) for q in near]


def enter(i, f, z, px, py, pd):
    barrier = pltpu.get_barrier_semaphore()

    def greet(**where):
        pl.semaphore_signal(barrier, inc=1, device_id=where, device_id_type=MESH)

    for p in (px, py, pd):
        greet(dp=p, feat=f)
    greet(dp=i, feat=f + 1 - 2 * (f % 2))

    @pl.when(z > 0)
    def _():
        greet(dp=i, feat=f - 2)

    @pl.when(z < LINE - 1)
    def _():
        greet(dp=i, feat=f + 2)

    pl.semaphore_wait(barrier, 5 + z * (LINE - 1 - z) // (LINE - 2))


def rcopy(src, dst, send, recv, **where):
    return pltpu.make_async_remote_copy(
        src_ref=src, dst_ref=dst, send_sem=send, recv_sem=recv, device_id=where, device_id_type=MESH
    )


def gather_kernel(
    tokens, cot, inv, weight, tok_all, cot_all, dense, pre, filled, wd, chunk, own, wsem, csem,
    a2a_s, a2a_r, up_s, dn_s, line_r, up2_s, dn2_s, line2_r, xy_s, xy_r, dg_s, dg_r, sib_s, sib_r,
):
    i, f, z, c, px, py, pd = place()
    half = tokens.shape[0] // 2
    order = line_order(z)
    sib = f + 1 - 2 * c
    local, slots, units, side = weight.shape
    per = wd.shape[2] // side
    load = pltpu.make_async_copy(weight, filled.at[:, pl.ds(0, slots)], own.at[2])
    load.start()
    filled[:, slots] = jnp.zeros((local, units, side), filled.dtype)
    enter(i, f, z, px, py, pd)

    def owner(q):
        return 2 * order[q // 2] + (c if q % 2 == 0 else 1 - c)

    def keep_dense(q):
        return pltpu.make_async_copy(wd.at[q], dense.at[owner(q)], wsem.at[q])

    def build(q):
        first = owner(q) * per

        def row(r, carry):
            at = pl.ds(pl.multiple_of(r * units, units), units)
            for b in range(per):
                wd[q, at, b * side : (b + 1) * side] = filled[r, inv[r, first + b]]
            return carry

        lax.fori_loop(0, local, row, 0)
        keep_dense(q).start()

    def forward(q):
        fetch = pltpu.make_async_copy(tok_all.at[:, owner(q)], chunk, csem)
        fetch.start()
        fetch.wait()
        pair = 2 * chunk.shape[1]

        def body(n, carry):
            lanes = pl.ds(pl.multiple_of(n * pair, pair), pair)
            x = chunk[pl.ds(2 * n, 2)].reshape(pair, chunk.shape[2])
            res = lax.dot_general(
                wd[q], x, (((1,), (1,)), ((), ())), preferred_element_type=jnp.float32
            )
            pre[:, lanes] = res if q == 0 else pre[:, lanes] + res
            return carry

        lax.fori_loop(0, chunk.shape[0] // 2, body, 0)

    mine = pltpu.make_async_copy(tokens, tok_all.at[i, f], own.at[0])
    mine.start()
    keep = pltpu.make_async_copy(cot.at[i], cot_all.at[i], own.at[1])
    keep.start()

    def blk(who, zp):
        return tok_all.at[who, 2 * zp + c]

    def src(k):
        return tokens if k == 0 else blk(i, order[k])

    def up(k):
        return rcopy(src(k), blk(i, order[k]), up_s.at[k], line_r.at[order[k]], dp=i, feat=f + 2)

    def down(k):
        return rcopy(src(k), blk(i, order[k]), dn_s.at[k], line_r.at[order[k]], dp=i, feat=f - 2)

    def up2(k):
        ref = blk(pd, order[k])
        return rcopy(ref, ref, up2_s.at[k], line2_r.at[order[k]], dp=i, feat=f + 2)

    def down2(k):
        ref = blk(pd, order[k])
        return rcopy(ref, ref, dn2_s.at[k], line2_r.at[order[k]], dp=i, feat=f - 2)

    def across(k, n):
        return rcopy(
            src(k), blk(i, order[k]), xy_s.at[n, k], xy_r.at[n, k], dp=(px, py)[n], feat=f
        )

    def corner(k, n):
        rows = pl.ds(n * half, half)
        ref = blk((px, py)[n], order[k]).at[rows]
        return rcopy(ref, ref, dg_s.at[n], dg_r.at[n], dp=(py, px)[n], feat=f)

    def twin(k, w):
        who = (i, px, py, pd)[w]
        ref = blk(who, order[k])
        s = src(k) if w == 0 else ref
        return rcopy(s, ref, sib_s.at[w, k], sib_r.at[w, k], dp=i, feat=sib)

    def exchange(n):
        p = (px, py, pd)[n]
        return rcopy(cot.at[p], cot_all.at[i], a2a_s.at[n], a2a_r.at[n], dp=p, feat=f)

    def goes_up(k):
        return jnp.logical_and(order[k] <= z, z < LINE - 1)

    def goes_down(k):
        return jnp.logical_and(order[k] >= z, z > 0)

    builds = ((0, 1), (2, 3), (4, 5), (6, 7))
    for k in range(LINE + 3):
        if k < LINE:
            if k > 0:
                pltpu.make_async_copy(
                    blk(i, order[k]), blk(i, order[k]), line_r.at[order[k]]
                ).wait()
            pl.when(goes_up(k))(lambda: up(k).start())
            pl.when(goes_down(k))(lambda: down(k).start())
            for n in range(2):
                across(k, n).start()
            twin(k, 0).start()
        if 1 <= k <= LINE:
            for n in range(2):
                across(k - 1, n).wait_recv()
                if k == 1:
                    corner(0, n).start()
                twin(k - 1, 1 + n).start()
        if 2 <= k < LINE + 2:
            if k == 2:
                for n in range(2):
                    corner(0, n).wait_recv()
            else:
                ref = blk(pd, order[k - 2])
                pltpu.make_async_copy(ref, ref, line2_r.at[order[k - 2]]).wait()
            pl.when(goes_up(k - 2))(lambda: up2(k - 2).start())
            pl.when(goes_down(k - 2))(lambda: down2(k - 2).start())
            twin(k - 2, 3).start()
        if k == 1:
            for n in range(3):
                exchange(n).start()
        if k == 0:
            load.wait()
        if k < len(builds):
            for q in builds[k]:
                build(q)
        if k == 2:
            mine.wait()
        if 2 <= k < LINE + 2:
            forward(2 * (k - 2))
        if k >= 3:
            for w in range(4):
                twin(k - 3, w).wait_recv()
            forward(2 * (k - 3) + 1)

    for n in range(3):
        exchange(n).wait()
    for q in range(2 * LINE):
        keep_dense(q).wait()
    keep.wait()
    for k in range(LINE):
        pl.when(goes_up(k))(lambda: up(k).wait_send())
        pl.when(goes_down(k))(lambda: down(k).wait_send())
        pl.when(goes_up(k))(lambda: up2(k).wait_send())
        pl.when(goes_down(k))(lambda: down2(k).wait_send())
        for n in range(2):
            across(k, n).wait_send()
            if k == 0:
                corner(k, n).wait_send()
        for w in range(4):
            twin(k, w).wait_send()


def local_kernel(cols, tok, pre, cot, hid, wgrad, grad_t, picked):
    step = pl.program_id(0)
    n, slots, units, side = wgrad.shape
    groups, _, rows, wide = tok.shape
    per = wide // side
    grads = []
    for a in range(n):
        for s in range(slots):
            b = cols[step * n + a, s]
            lanes = pl.ds(pl.multiple_of((b % per) * side, side), side)
            for g in range(groups):
                picked[a % 2, g * rows : (g + 1) * rows, s * side : (s + 1) * side] = tok[
                    g, b // per, :, lanes
                ]
        x = picked.at[a % 2]
        v = pre[a * units : (a + 1) * units, :]
        k0, k1 = 0.7978845608028654, 0.044715
        th = jnp.tanh(k0 * (v + k1 * v * v * v))
        act = (0.5 * v * (1.0 + th)).astype(jnp.bfloat16)
        slope = 0.5 * (1.0 + th) + 0.5 * v * (1.0 - th * th) * (k0 * (1.0 + 3.0 * k1 * v * v))
        ct = jnp.concatenate([cot[g, a] for g in range(groups)], axis=1).astype(jnp.float32)
        grad = ct * slope
        grads.append(grad)
        grad = grad.astype(jnp.bfloat16)
        for g in range(groups):
            hid[g, a] = act[:, g * rows : (g + 1) * rows]
        wg = jnp.dot(grad, x[...], preferred_element_type=jnp.float32).astype(jnp.bfloat16)
        for s in range(slots):
            wgrad[a, s] = wg[:, s * side : (s + 1) * side]
    grad_t[...] = jnp.concatenate(grads, axis=0).T.astype(jnp.bfloat16)


def scatter_kernel(
    grad_t, wd, hid, out, hid_all, wbuf, part, sibbuf, xhalf, yhalf, xfull, yfull, upbuf, dnbuf,
    up2buf, dn2buf, own, wsem, a2a_s, a2a_r, sib_s, sib_r, half_s, half_r, full_s, full_r, up_s, up_r, dn_s, dn_r,
    up2_s, up2_r, dn2_s, dn2_r,
):
    i, f, z, c, px, py, pd = place()
    groups, rows, wide = sibbuf.shape[1:]
    half = rows // 2
    order = line_order(z)[::-1]
    sib = f + 1 - 2 * c
    tile = 256

    def fetch(q):
        k, own_side = q // 2, q % 2
        col = 2 * order[k] + (c if own_side else 1 - c)
        return pltpu.make_async_copy(wd.at[col], wbuf.at[q % 2], wsem.at[q % 2])

    fetch(0).start()
    enter(i, f, z, px, py, pd)
    keep = pltpu.make_async_copy(hid.at[i], hid_all.at[i], own)
    keep.start()

    def exchange(n):
        p = (px, py, pd)[n]
        return rcopy(hid.at[p], hid_all.at[i], a2a_s.at[n], a2a_r.at[n], dp=p, feat=f)

    def work(q):
        k = q // 2
        fetch(q).wait()
        if q + 1 < 2 * LINE:
            fetch(q + 1).start()

        def body(n, carry):
            lanes = pl.ds(pl.multiple_of(n * tile, tile), tile)
            res = jnp.dot(
                grad_t[...], wbuf[q % 2, :, lanes], preferred_element_type=jnp.float32
            ).astype(jnp.bfloat16)
            for g in range(groups):
                part[q % 2, k, g, :, lanes] = res[g * rows : (g + 1) * rows]
            return carry

        lax.fori_loop(0, wide // tile, body, 0)

    def add(dst, *others):
        def body(n, carry):
            at = pl.ds(pl.multiple_of(n * 16, 16), 16)
            total = dst[at].astype(jnp.float32)
            for o in others:
                total = total + o[at].astype(jnp.float32)
            dst[at] = total.astype(jnp.bfloat16)
            return carry

        lax.fori_loop(0, dst.shape[0] // 16, body, 0)

    def twin(k):
        return rcopy(part.at[0, k], sibbuf.at[k], sib_s.at[k], sib_r.at[k], dp=i, feat=sib)

    first, second = pl.ds(0, half), pl.ds(half, half)

    def corner(k, n):
        rows_n = (first, second)[n]
        return rcopy(
            part.at[1, k, pd, rows_n], (xhalf, yhalf)[n], half_s.at[n], half_r.at[n],
            dp=(px, py)[n], feat=f,
        )

    def across(k, n):
        p = (px, py)[n]
        return rcopy(
            part.at[1, k, p], (xfull, yfull)[n].at[k], full_s.at[n, k], full_r.at[n, k],
            dp=p, feat=f,
        )

    def up(k):
        return rcopy(
            part.at[1, k, i], upbuf.at[order[k]], up_s.at[k], up_r.at[order[k]], dp=i, feat=f + 2
        )

    def down(k):
        return rcopy(
            part.at[1, k, i], dnbuf.at[order[k]], dn_s.at[k], dn_r.at[order[k]], dp=i, feat=f - 2
        )

    def up2(k):
        return rcopy(
            part.at[1, k, pd], up2buf.at[order[k]], up2_s.at[k], up2_r.at[order[k]], dp=i, feat=f + 2
        )

    def down2(k):
        return rcopy(
            part.at[1, k, pd], dn2buf.at[order[k]], dn2_s.at[k], dn2_r.at[order[k]], dp=i, feat=f - 2
        )

    def got(buf, sem, k):
        ref = buf.at[order[k]]
        pltpu.make_async_copy(ref, ref, sem.at[order[k]]).wait()

    def from_below(k):
        return jnp.logical_and(order[k] >= z, z > 0)

    def from_above(k):
        return jnp.logical_and(order[k] <= z, z < LINE - 1)

    def collect(k, mine, ups, downs):
        @pl.when(from_below(k))
        def _():
            got(ups[0], ups[1], k)
            add(mine, ups[0].at[order[k]])

        @pl.when(from_above(k))
        def _():
            got(downs[0], downs[1], k)
            add(mine, downs[0].at[order[k]])

    last = LINE - 1
    for step in range(LINE + 2):
        k = step
        if k < LINE:
            work(2 * k)
            twin(k).start()
            work(2 * k + 1)
            if k == 0:
                for n in range(3):
                    exchange(n).start()
            twin(k).wait_recv()
            add(part.at[1, k, pd], sibbuf.at[k, pd])
            for n, g in ((0, px), (1, py)):
                add(part.at[1, k, g], sibbuf.at[k, g])
                if k < last:
                    across(k, n).start()
            add(part.at[1, k, i], sibbuf.at[k, i])
            collect(k, part.at[1, k, pd], (up2buf, up2_r), (dn2buf, dn2_r))
            if k < last:
                pl.when(order[k] > z)(lambda: up2(k).start())
                pl.when(order[k] < z)(lambda: down2(k).start())
            else:
                corner(k, 0).start()
                corner(k, 1).start()
        k = step - 1
        if 0 <= k < LINE:
            if k == last:
                corner(k, 0).wait_recv()
                add(part.at[1, k, py, first], xhalf)
                across(k, 1).start()
                corner(k, 1).wait_recv()
                add(part.at[1, k, px, second], yhalf)
                across(k, 0).start()
            else:
                across(k, 0).wait_recv()
                across(k, 1).wait_recv()
                add(part.at[1, k, i], xfull.at[k], yfull.at[k])
                collect(k, part.at[1, k, i], (upbuf, up_r), (dnbuf, dn_r))
                pl.when(order[k] > z)(lambda: up(k).start())
                pl.when(order[k] < z)(lambda: down(k).start())
        if step == LINE + 1:
            collect(last, part.at[1, last, i], (upbuf, up_r), (dnbuf, dn_r))
            across(last, 0).wait_recv()
            across(last, 1).wait_recv()
            add(part.at[1, last, i], xfull.at[last], yfull.at[last])

    done = pltpu.make_async_copy(part.at[1, LINE - 1, i], out, wsem.at[0])
    done.start()
    for n in range(3):
        exchange(n).wait()
    keep.wait()
    for k in range(LINE):
        twin(k).wait_send()
        for n in range(2):
            if k == last:
                corner(k, n).wait_send()
            across(k, n).wait_send()
        if k < last:
            pl.when(order[k] > z)(lambda: up(k).wait_send())
            pl.when(order[k] < z)(lambda: down(k).wait_send())
            pl.when(order[k] > z)(lambda: up2(k).wait_send())
            pl.when(order[k] < z)(lambda: down2(k).wait_send())
    done.wait()


def token_plan(tokens, columns, weight, cotangent):
    rows, wide = tokens.shape
    local, slots, units, side = weight.shape
    n_dp, n_feat = lax.axis_size("dp"), lax.axis_size("feat")
    bf = jnp.bfloat16
    dma = pltpu.SemaphoreType.DMA
    anywhere = pl.BlockSpec(memory_space=pl.ANY)
    inside = pl.BlockSpec(memory_space=pltpu.VMEM)
    blocks = n_feat * wide // side
    total = n_dp * rows

    cot_t = cotangent.reshape(rows, local, n_dp, units).transpose(2, 1, 3, 0)
    hit = columns[:, :, None] == jnp.arange(blocks, dtype=jnp.int32)
    inv = jnp.min(jnp.where(hit, jnp.arange(slots, dtype=jnp.int32)[:, None], slots), axis=1)
    tok_all, cot_all, dense, pre = pl.pallas_call(
        gather_kernel,
        out_shape=(
            jax.ShapeDtypeStruct((n_dp, n_feat, rows, wide), bf),
            jax.ShapeDtypeStruct(cot_t.shape, bf),
            jax.ShapeDtypeStruct((n_feat, local * units, wide), bf),
            jax.ShapeDtypeStruct((local * units, total), jnp.float32),
        ),
        in_specs=[anywhere, anywhere, pl.BlockSpec(memory_space=pltpu.SMEM), anywhere],
        out_specs=(anywhere, anywhere, anywhere, inside),
        scratch_shapes=[
            pltpu.VMEM((local, slots + 1, units, side), bf),
            pltpu.VMEM((n_feat, local * units, wide), bf),
            pltpu.VMEM((n_dp, rows, wide), bf),
            dma((3,)), dma((n_feat,)), dma(()),
            dma((3,)), dma((3,)), dma((LINE,)), dma((LINE,)), dma((LINE,)),
            dma((LINE,)), dma((LINE,)), dma((LINE,)),
            dma((2, LINE)), dma((2, LINE)), dma((2,)), dma((2,)),
            dma((4, LINE)), dma((4, LINE)),
        ],
        compiler_params=pltpu.CompilerParams(
            collective_id=0, has_side_effects=True, vmem_limit_bytes=56 * 2**20
        ),
        name="gather",
    )(tokens, cot_t, inv, weight)

    n = side // units
    hid_t, weight_grad, grad_t = pl.pallas_call(
        local_kernel,
        out_shape=(
            jax.ShapeDtypeStruct(cot_t.shape, bf),
            jax.ShapeDtypeStruct(weight.shape, bf),
            jax.ShapeDtypeStruct((total, local * units), bf),
        ),
        grid_spec=pltpu.PrefetchScalarGridSpec(
            num_scalar_prefetch=1,
            grid=(local // n,),
            in_specs=[
                inside,
                pl.BlockSpec((n * units, total), lambda r, c: (r, 0)),
                pl.BlockSpec((n_dp, n, units, rows), lambda r, c: (0, r, 0, 0)),
            ],
            out_specs=(
                pl.BlockSpec((n_dp, n, units, rows), lambda r, c: (0, r, 0, 0)),
                pl.BlockSpec((n, slots, units, side), lambda r, c: (r, 0, 0, 0)),
                pl.BlockSpec((total, n * units), lambda r, c: (0, r)),
            ),
            scratch_shapes=[pltpu.VMEM((2, total, slots * side), bf)],
        ),
        compiler_params=pltpu.CompilerParams(vmem_limit_bytes=48 * 2**20),
        name="local",
    )(columns, tok_all, pre, cot_all)

    input_grad, hid_all = pl.pallas_call(
        scatter_kernel,
        out_shape=(
            jax.ShapeDtypeStruct((rows, wide), bf),
            jax.ShapeDtypeStruct(cot_t.shape, bf),
        ),
        in_specs=[inside, anywhere, anywhere],
        out_specs=(anywhere,) * 2,
        scratch_shapes=[
            pltpu.VMEM((2, local * units, wide), bf),
            pltpu.VMEM((2, LINE, n_dp, rows, wide), bf),
            pltpu.VMEM((LINE, n_dp, rows, wide), bf),
            pltpu.VMEM((rows // 2, wide), bf),
            pltpu.VMEM((rows // 2, wide), bf),
            pltpu.VMEM((LINE, rows, wide), bf),
            pltpu.VMEM((LINE, rows, wide), bf),
            pltpu.VMEM((LINE, rows, wide), bf),
            pltpu.VMEM((LINE, rows, wide), bf),
            pltpu.VMEM((LINE, rows, wide), bf),
            pltpu.VMEM((LINE, rows, wide), bf),
            dma(()), dma((2,)), dma((3,)), dma((3,)), dma((LINE,)), dma((LINE,)),
            dma((2,)), dma((2,)), dma((2, LINE)), dma((2, LINE)),
            dma((LINE,)), dma((LINE,)), dma((LINE,)), dma((LINE,)),
            dma((LINE,)), dma((LINE,)), dma((LINE,)), dma((LINE,)),
        ],
        compiler_params=pltpu.CompilerParams(
            collective_id=1, has_side_effects=True, vmem_limit_bytes=56 * 2**20
        ),
        name="scatter",
    )(grad_t, dense, hid_t)
    hidden = hid_all.transpose(3, 1, 0, 2).reshape(rows, local * side)
    return (hidden, input_grad, weight_grad)


def solution(mesh):
    in_specs = (P("dp", "feat"), P("feat", None), P("feat", None, "dp", None), P("dp", "feat"))
    out_specs = (P("dp", "feat"), P("dp", "feat"), P("feat", None, "dp", None))
    square = mesh.shape["dp"] == 4 and mesh.shape["feat"] == 2 * LINE
    return jax.shard_map(
        token_plan if square else on_device,
        mesh=mesh, in_specs=in_specs, out_specs=out_specs, check_vma=False,
    )
```
